32 devices in a mesh: groups: 2 (over y), doc: 8 (over z, x), layer: 2 (over core).
Axes of the slice: x: 2, y: 2, z: 4, core: 2. Of those that a mesh axis runs over, the one named last changes fastest.
Arguments:
- queries: bfloat16 [2, 2, 4096, 768], P('layer', None, 'doc', 'groups'), parts along dimension 3, may hold values from -6 to 6
- inverse_fisher: bfloat16 [2, 2, 4096, 4096], P('layer', None, 'doc'), as said below
- documents: bfloat16 [2, 3584, 2, 4096], P('layer', ('groups', 'doc')), parts along dimension 1, may hold values from -0.0625 to 0.0625
- doc_order: int32 [16, 224], P(('groups', 'doc')), parts along dimension 0, may hold values from 0 to 223, each once within a row
Outputs:
- influence: float32 [3584, 384], P(('groups', 'doc')), parts along dimension 0
The draws below stay inside these ranges and needn't reach their ends.
There are 2 independent parts, one for each index of `groups`. The reference program is written for one: setup_inputs(seed, part) draws one part's arguments, and reference() takes and returns one part's arrays. A program takes and returns all parts, laid end to end along the dimension named above; an argument that names none is the same for every part. Nothing has to cross between parts.
Inputs may be any that keep to these rules, and one draw needn't show every extreme that they name: Each row of doc_order holds every number of 0 to 223 once. inverse_fisher[l, m] is symmetric.
All inputs are finite; a program needn't handle non-finite values.
Results may differ from the reference program's by a relative error of at most 0.0029.
Values may be sent and summed in bfloat16 or wider, within the bound.
No kernel may reach another device: no remote copies, remote signals or barrier semaphores. Data moves between devices by JAX's collectives and lax.ppermute only.
A program may use at most 64 MiB of HBM per device.

```python
import math
import jax
import jax.numpy as jnp

K = 4096
M = 2
Q = 384
DOC_DEV = 224
LAYERS = 2
SLABS = 8
DOCS = 1792


def draw_inverse_fisher(key, part):
    key = jax.random.fold_in(key, 11)
    key_diag, key_noise = jax.random.split(key)
    diagonal = jnp.exp(jax.random.uniform(key_diag, (LAYERS, M, K), jnp.float32, math.log(0.5), math.log(2.0)))
    noise = jax.random.normal(key_noise, (LAYERS, M, K, K), jnp.float32) * (0.35 / math.sqrt(K))
    symmetric = noise + jnp.swapaxes(noise, -1, -2)
    rows = lax_iota_rows()
    eye = (rows[:, None] == rows[None, :]).astype(jnp.float32)
    return (symmetric + eye * diagonal[..., None]).astype(jnp.bfloat16)


def lax_iota_rows():
    return jnp.arange(K, dtype=jnp.int32)


def level_of(own_key, dims, cuts, low, top_value):
    level = 1.0
    for axis_at, parts in cuts:
        steps = jax.random.uniform(jax.random.fold_in(jax.random.fold_in(own_key, 6), axis_at), (parts,), jnp.float32, low / len(cuts), top_value / len(cuts))
        level = level * jnp.repeat(jnp.exp(steps), dims[axis_at] // parts).reshape((-1,) + (1,) * (len(dims) - 1 - axis_at))
    return level


def normal_values(key, extent, spread, bound, cuts=(), held_as=jnp.bfloat16):
    gain = level_of(key, extent, cuts, -0.22, 0.18) if cuts else 1.0
    entries = jax.random.normal(key, extent, jnp.float32) * spread * gain
    return jnp.minimum(jnp.maximum(entries, -bound), bound).astype(held_as)


def setup_inputs(seed: int = 0, part: int = 0) -> dict:
    keys = jax.random.split(jax.random.key(seed), 5)
    own_keys = jax.random.split(jax.random.fold_in(keys[4], part), 5)
    queries = normal_values(own_keys[0], (LAYERS, M, K, Q), 1.0, 6.0, ((0, 2), (2, 8)))
    inverse_fisher = draw_inverse_fisher(jax.random.fold_in(keys[4], 71), part)
    documents = normal_values(own_keys[2], (LAYERS, DOCS, M, K), (M * K) ** -0.5, 0.0625, ((0, 2), (1, 8)))
    doc_order = jax.vmap(lambda own: jax.random.permutation(own, DOC_DEV))(jax.random.split(own_keys[3], SLABS)).reshape((SLABS, DOC_DEV)).astype(jnp.int32)
    return {"queries": queries, "inverse_fisher": inverse_fisher, "documents": documents, "doc_order": doc_order}


def place_rows(rows, order):
    return jnp.zeros_like(rows).at[order].set(rows)


def reference(queries, inverse_fisher, documents, doc_order):
    total = jnp.zeros((DOCS, Q), jnp.float32)
    for layer in range(LAYERS):
        blocks = []
        for module in range(M):
            fisher = inverse_fisher[layer, module].astype(jnp.float32)
            query_block = queries[layer, module].astype(jnp.float32)
            blocks.append(jnp.dot(fisher, query_block, preferred_element_type=jnp.float32).astype(jnp.bfloat16))
        precond = jnp.stack(blocks)
        flat_store = documents[layer].reshape(DOCS, M * K)
        total = total + jnp.dot(flat_store, precond.reshape(M * K, Q), preferred_element_type=jnp.float32)
    slabs = total.reshape(SLABS, DOC_DEV, Q)
    return jax.vmap(place_rows)(slabs, doc_order).reshape(DOCS, Q)
```

```python
import jax
import jax.numpy as jnp
import numpy as np
from jax import lax
from jax.sharding import PartitionSpec as P


def ring_order(n):
    half = n // 2
    return [2 * i for i in range(half)] + [2 * i + 1 for i in reversed(range(half))]


def dot(a, b):
    return jnp.dot(a, b, preferred_element_type=jnp.float32)


def place_documents(store, order):
    n_rows = store.shape[0]
    place = (order[None, :] == lax.broadcasted_iota(jnp.int32, (n_rows, n_rows), 0)).astype(store.dtype)
    return dot(place, store.reshape(n_rows, -1)).astype(store.dtype)


def make_per_device(n):
    ring = ring_order(n)
    where = np.zeros(n, np.int32)
    where[ring] = np.arange(n)
    up = [(ring[i], ring[(i + 1) % n]) for i in range(n)]
    down = [(b, a) for a, b in up]

    def ring_gather(blocks, use):
        m_all = len(blocks)
        for m in range(m_all):
            use(m, blocks[m], 0)
        going_up, going_down = list(blocks), list(blocks)
        for step in range(1, n // 2 + 1):
            for m in range(m_all):
                last = step == n // 2
                if not last or m % 2 == 0:
                    going_up[m] = lax.ppermute(going_up[m], "doc", up)
                    use(m, going_up[m], step)
                if not last or m % 2 == 1:
                    going_down[m] = lax.ppermute(going_down[m], "doc", down)
                    use(m, going_down[m], -step)

    def per_device(queries, inverse_fisher, documents, doc_order):
        fisher = inverse_fisher[0]
        query = queries[0]
        modules, depth, width = fisher.shape
        at = jnp.asarray(where)[lax.axis_index("doc")]
        ring_of = jnp.asarray(np.asarray(ring, np.int32))

        def first(shift):
            return ring_of[(at - shift + n) % n] * depth

        placed = place_documents(documents[0], doc_order[0])
        acc = [None] * modules

        def add_precond(m, block, shift):
            part = dot(lax.dynamic_slice_in_dim(fisher[m], first(shift), depth, 1), block)
            acc[m] = part if acc[m] is None else acc[m] + part

        ring_gather([query[m] for m in range(modules)], add_precond)
        precond = [a.astype(jnp.bfloat16) for a in acc]
        score = [None]

        def add_score(m, block, shift):
            part = dot(lax.dynamic_slice_in_dim(placed, m * width + first(shift), depth, 1), block)
            score[0] = part if score[0] is None else score[0] + part

        ring_gather(precond, add_score)
        return score[0] + lax.ppermute(score[0], "layer", [(0, 1), (1, 0)])

    return per_device


def per_device_any(queries, inverse_fisher, documents, doc_order):
    fisher = inverse_fisher[0]
    placed = place_documents(documents[0], doc_order[0])
    full_queries = lax.all_gather(queries[0], "doc", axis=1, tiled=True)
    precond = jnp.einsum("mji,miq->mjq", fisher, full_queries, preferred_element_type=jnp.float32).astype(jnp.bfloat16)
    full_precond = lax.all_gather(precond, "doc", axis=1, tiled=True)
    score = dot(placed, full_precond.reshape(-1, full_precond.shape[2]))
    return lax.psum(score, "layer")


def solution(mesh):
    n = mesh.shape["doc"]
    per_device = make_per_device(n) if n == 8 and mesh.shape["layer"] == 2 else per_device_any
    in_specs = (
        P("layer", None, "doc", "groups"),
        P("layer", None, "doc", None),
        P("layer", ("groups", "doc"), None, None),
        P(("groups", "doc"), None),
    )
    out_specs = P(("groups", "doc"), None)
    return jax.shard_map(per_device, mesh=mesh, in_specs=in_specs, out_specs=out_specs, check_vma=False)
```

```python
import functools

import jax
import jax.numpy as jnp
import numpy as np
from jax import lax
from jax.experimental import pallas as pl
from jax.experimental.pallas import tpu as pltpu
from jax.sharding import PartitionSpec as P

VMEM_LIMIT = 40 * 1024 * 1024


def dot(a, b):
    return jnp.dot(a, b, preferred_element_type=jnp.float32)


def ring_order(n):
    half = n // 2
    return [2 * i for i in range(half)] + [2 * i + 1 for i in reversed(range(half))]


def precond_kernel(count, has_acc, table, *refs):
    del table
    fisher, blocks = refs[:count], refs[count : 2 * count]
    total = refs[2 * count][...] if has_acc else None
    out = refs[-1]
    for f, block in zip(fisher, blocks):
        part = dot(f[0], block[...])
        total = part if total is None else total + part
    out[...] = total.astype(out.dtype)


def add_precond(table, fisher, m, entries, acc, dtype):
    _, depth, _ = fisher.shape
    width = entries[0][1].shape[1]
    whole = pl.BlockSpec((depth, width), lambda i, t: (0, 0))
    in_specs = [pl.BlockSpec((1, depth, depth), lambda i, t, k=k: (m, 0, t[k])) for k, _ in entries]
    in_specs += [whole] * (len(entries) + (acc is not None))
    operands = [fisher] * len(entries) + [a for _, a in entries] + ([acc] if acc is not None else [])
    return pl.pallas_call(
        functools.partial(precond_kernel, len(entries), acc is not None),
        out_shape=jax.ShapeDtypeStruct((depth, width), dtype),
        grid_spec=pltpu.PrefetchScalarGridSpec(num_scalar_prefetch=1, grid=(1,), in_specs=in_specs, out_specs=whole),
        compiler_params=pltpu.CompilerParams(vmem_limit_bytes=VMEM_LIMIT),
        cost_estimate=pl.CostEstimate(
            flops=2 * depth * depth * width * len(entries),
            bytes_accessed=depth * (depth + 2 * width) * 2 * len(entries),
            transcendentals=0,
        ),
    )(table, *operands)


def place_kernel(table, order, docs, *refs):
    del table
    out = refs[-1]
    rows = order.shape[1]
    put = jnp.where(order[...] == lax.broadcasted_iota(jnp.int32, (rows, rows), 0), 1.0, 0.0).astype(jnp.bfloat16)
    out[0] = dot(put, docs[0]).astype(out.dtype)


def place(table, order, docs, depth, after):
    modules, rows, width = docs.shape
    return pl.pallas_call(
        place_kernel,
        out_shape=jax.ShapeDtypeStruct(docs.shape, docs.dtype),
        grid_spec=pltpu.PrefetchScalarGridSpec(
            num_scalar_prefetch=1,
            grid=(modules, width // depth),
            in_specs=[pl.BlockSpec((1, rows), lambda m, i, t: (0, 0))]
            + [pl.BlockSpec((1, rows, depth), lambda m, i, t: (m, 0, t[i]))]
            + [pl.BlockSpec(memory_space=pl.ANY)] * len(after),
            out_specs=pl.BlockSpec((1, rows, depth), lambda m, i, t: (m, 0, i)),
        ),
        compiler_params=pltpu.CompilerParams(vmem_limit_bytes=VMEM_LIMIT),
        cost_estimate=pl.CostEstimate(flops=2 * docs.size * rows, bytes_accessed=4 * docs.size, transcendentals=0),
    )(table, order, docs, *after)


def per_device_plane(queries, inverse_fisher, documents, doc_order):
    fisher = inverse_fisher[0]
    modules, depth, width = fisher.shape
    n = width // depth
    ring = ring_order(n)
    up = [(ring[i], ring[(i + 1) % n]) for i in range(n)]
    down = [(b, a) for a, b in up]
    owners = np.zeros((n, n), np.int32)
    for i, d in enumerate(ring):
        owners[d] = [ring[(i - shift) % n] for shift in range(n)]
    table = jnp.asarray(owners)[lax.axis_index("doc")]
    docs = jnp.swapaxes(documents[0], 0, 1)

    def ring_gather(blocks, state, use):
        going = [[block, block] for block in blocks]
        fresh = [[(0, block)] for block in blocks]
        for step in range(1, n // 2 + 1):
            for m in range(modules):
                if step > 1:
                    going[m], state[m] = lax.optimization_barrier((going[m], state[m]))
                arrivals = []
                last = step == n // 2
                if not last or m % 2 == 0:
                    going[m][0] = lax.ppermute(going[m][0], "doc", up)
                    arrivals.append((step, going[m][0]))
                if not last or m % 2 == 1:
                    going[m][1] = lax.ppermute(going[m][1], "doc", down)
                    arrivals.append((n - step, going[m][1]))
                state[m] = use(m, state[m], fresh[m], False)
                fresh[m] = arrivals
        return [use(m, state[m], fresh[m], True) for m in range(modules)]

    third = []

    def add_query(m, acc, arrivals, last):
        third.append(arrivals[0][1])
        return add_precond(table, fisher, m, arrivals, acc, jnp.bfloat16 if last else jnp.float32)

    precond = ring_gather([queries[0, m] for m in range(modules)], [None] * modules, add_query)
    placed = place(table, doc_order, docs, depth, [third[2 * modules]])

    def add_score(m, score, arrivals, last):
        for shift, block in arrivals:
            part = dot(placed[m][:, shift * depth : (shift + 1) * depth], block)
            score = part if score is None else score + part
        return score

    score = sum(ring_gather(precond, [None] * modules, add_score))
    return score + lax.ppermute(score, "layer", [(0, 1), (1, 0)])


def per_device_any(queries, inverse_fisher, documents, doc_order):
    fisher = inverse_fisher[0]
    n_rows = documents.shape[1]
    put = (doc_order == lax.broadcasted_iota(jnp.int32, (n_rows, n_rows), 0)).astype(documents.dtype)
    placed = dot(put, documents[0].reshape(n_rows, -1)).astype(documents.dtype)
    full_queries = lax.all_gather(queries[0], "doc", axis=1, tiled=True)
    precond = jnp.einsum("mji,miq->mjq", fisher, full_queries, preferred_element_type=jnp.float32).astype(jnp.bfloat16)
    full_precond = lax.all_gather(precond, "doc", axis=1, tiled=True)
    score = dot(placed, full_precond.reshape(-1, full_precond.shape[2]))
    return lax.psum(score, "layer")


def solution(mesh):
    plane = mesh.shape["doc"] == 8 and mesh.shape["layer"] == 2
    in_specs = (
        P("layer", None, "doc", "groups"),
        P("layer", None, "doc", None),
        P("layer", ("groups", "doc"), None, None),
        P(("groups", "doc"), None),
    )
    return jax.shard_map(
        per_device_plane if plane else per_device_any,
        mesh=mesh,
        in_specs=in_specs,
        out_specs=P(("groups", "doc"), None),
        check_vma=False,
    )
```

```python
import functools

import jax
import jax.numpy as jnp
import numpy as np
from jax import lax
from jax.experimental import pallas as pl
from jax.experimental.pallas import tpu as pltpu
from jax.sharding import PartitionSpec as P

VMEM_LIMIT = 16 * 1024 * 1024


def dot(a, b):
    return jnp.dot(a, b, preferred_element_type=jnp.float32)


def ring_order(n):
    half = n // 2
    return [2 * i for i in range(half)] + [2 * i + 1 for i in reversed(range(half))]


def precond_kernel(count, has_acc, table, *refs):
    del table
    fisher, blocks = refs[:count], refs[count : 2 * count]
    total = refs[2 * count][...] if has_acc else None
    out = refs[-1]
    for f, block in zip(fisher, blocks):
        part = dot(f[0], block[...])
        total = part if total is None else total + part
    out[...] = total.astype(out.dtype)


def add_precond(table, fisher, m, entries, acc, dtype):
    _, depth, _ = fisher.shape
    width = entries[0][1].shape[1]
    whole = pl.BlockSpec((depth, width), lambda i, t: (0, 0))
    in_specs = [pl.BlockSpec((1, depth, depth), lambda i, t, k=k: (m, 0, t[k])) for k, _ in entries]
    in_specs += [whole] * (len(entries) + (acc is not None))
    operands = [fisher] * len(entries) + [a for _, a in entries] + ([acc] if acc is not None else [])
    return pl.pallas_call(
        functools.partial(precond_kernel, len(entries), acc is not None),
        out_shape=jax.ShapeDtypeStruct((depth, width), dtype),
        grid_spec=pltpu.PrefetchScalarGridSpec(num_scalar_prefetch=1, grid=(1,), in_specs=in_specs, out_specs=whole),
        compiler_params=pltpu.CompilerParams(vmem_limit_bytes=VMEM_LIMIT),
        cost_estimate=pl.CostEstimate(
            flops=2 * depth * depth * width * len(entries),
            bytes_accessed=depth * (depth + 2 * width) * 2 * len(entries),
            transcendentals=0,
        ),
    )(table, *operands)


def place_kernel(table, order, docs, out):
    del table
    rows = order.shape[1]
    put = jnp.where(order[...] == lax.broadcasted_iota(jnp.int32, (rows, rows), 0), 1.0, 0.0).astype(jnp.bfloat16)
    out[...] = dot(put, docs[0]).astype(out.dtype)


def place(table, order, docs, depth, m):
    _, rows, width = docs.shape
    return pl.pallas_call(
        place_kernel,
        out_shape=jax.ShapeDtypeStruct((rows, width), docs.dtype),
        grid_spec=pltpu.PrefetchScalarGridSpec(
            num_scalar_prefetch=1,
            grid=(width // depth,),
            in_specs=[
                pl.BlockSpec((1, rows), lambda i, t: (0, 0)),
                pl.BlockSpec((1, rows, depth), lambda i, t: (m, 0, t[i])),
            ],
            out_specs=pl.BlockSpec((rows, depth), lambda i, t: (0, i)),
        ),
        compiler_params=pltpu.CompilerParams(vmem_limit_bytes=VMEM_LIMIT),
        cost_estimate=pl.CostEstimate(flops=2 * rows * rows * width, bytes_accessed=4 * rows * width, transcendentals=0),
    )(table, order, docs)


def per_device_plane(queries, inverse_fisher, documents, doc_order):
    fisher = inverse_fisher[0]
    modules, depth, width = fisher.shape
    n = width // depth
    ring = ring_order(n)
    up = [(ring[i], ring[(i + 1) % n]) for i in range(n)]
    down = [(b, a) for a, b in up]
    owners = np.zeros((n, n), np.int32)
    for i, d in enumerate(ring):
        owners[d] = [ring[(i - shift) % n] for shift in range(n)]
    table = jnp.asarray(owners)[lax.axis_index("doc")]
    docs = jnp.swapaxes(documents[0], 0, 1)

    def ring_gather(blocks, state, use, waits):
        going = [[block, block] for block in blocks]
        fresh = [[(0, block)] for block in blocks]
        for step in range(1, n // 2 + 1):
            for m in range(modules):
                if step > 1:
                    going[m], state[m], _ = lax.optimization_barrier((going[m], state[m], waits.get((step, m), ())))
                arrivals = []
                last = step == n // 2
                if not last or m % 2 == 0:
                    going[m][0] = lax.ppermute(going[m][0], "doc", up)
                    arrivals.append((step, going[m][0]))
                if not last or m % 2 == 1:
                    going[m][1] = lax.ppermute(going[m][1], "doc", down)
                    arrivals.append((n - step, going[m][1]))
                state[m] = use(m, state[m], fresh[m], False)
                fresh[m] = arrivals
        return [use(m, state[m], fresh[m], True) for m in range(modules)]

    def add_query(m, acc, arrivals, last):
        return add_precond(table, fisher, m, arrivals, acc, jnp.bfloat16 if last else jnp.float32)

    blocks = [queries[0, 0]]
    for m in range(1, modules):
        blocks.append(lax.optimization_barrier((queries, blocks[-1]))[0][0, m])
    placed = [place(table, doc_order, docs, depth, m) for m in range(modules)]
    waits = {(2, modules - 1): docs, (3, 0): placed[0], (3, modules - 1): placed[1:]}
    precond = ring_gather(blocks, [None] * modules, add_query, waits)

    def add_score(m, score, arrivals, last):
        for shift, block in arrivals:
            part = dot(placed[m][:, shift * depth : (shift + 1) * depth], block)
            score = part if score is None else score + part
        return score

    score = sum(ring_gather(precond, [None] * modules, add_score, {}))
    return score + lax.ppermute(score, "layer", [(0, 1), (1, 0)])


def per_device_any(queries, inverse_fisher, documents, doc_order):
    fisher = inverse_fisher[0]
    n_rows = documents.shape[1]
    put = (doc_order == lax.broadcasted_iota(jnp.int32, (n_rows, n_rows), 0)).astype(documents.dtype)
    placed = dot(put, documents[0].reshape(n_rows, -1)).astype(documents.dtype)
    full_queries = lax.all_gather(queries[0], "doc", axis=1, tiled=True)
    precond = jnp.einsum("mji,miq->mjq", fisher, full_queries, preferred_element_type=jnp.float32).astype(jnp.bfloat16)
    full_precond = lax.all_gather(precond, "doc", axis=1, tiled=True)
    score = dot(placed, full_precond.reshape(-1, full_precond.shape[2]))
    return lax.psum(score, "layer")


def solution(mesh):
    plane = mesh.shape["doc"] == 8 and mesh.shape["layer"] == 2
    in_specs = (
        P("layer", None, "doc", "groups"),
        P("layer", None, "doc", None),
        P("layer", ("groups", "doc"), None, None),
        P(("groups", "doc"), None),
    )
    return jax.shard_map(
        per_device_plane if plane else per_device_any,
        mesh=mesh,
        in_specs=in_specs,
        out_specs=P(("groups", "doc"), None),
        check_vma=False,
    )
```

```python
import functools

import jax
import jax.numpy as jnp
import numpy as np
from jax import lax
from jax.experimental import pallas as pl
from jax.experimental.pallas import tpu as pltpu
from jax.sharding import PartitionSpec as P

VMEM_LIMIT = 16 * 1024 * 1024


def dot(a, b):
    return jnp.dot(a, b, preferred_element_type=jnp.float32)


def ring_order(n):
    half = n // 2
    return [2 * i for i in range(half)] + [2 * i + 1 for i in reversed(range(half))]


def precond_kernel(count, has_acc, table, *refs):
    del table
    fisher, blocks = refs[:count], refs[count : 2 * count]
    total = refs[2 * count][...] if has_acc else None
    out = refs[-1]
    for f, block in zip(fisher, blocks):
        part = dot(f[0], block[...])
        total = part if total is None else total + part
    out[...] = total.astype(out.dtype)


def add_precond(table, fisher, m, entries, acc, dtype):
    _, depth, _ = fisher.shape
    width = entries[0][2].shape[1]
    whole = pl.BlockSpec((depth, width), lambda i, t: (0, 0))
    in_specs = [
        pl.BlockSpec((1, depth, b.shape[0]), lambda i, t, k=k, h=h, parts=depth // b.shape[0]: (m, 0, t[k] * parts + h))
        for k, h, b in entries
    ]
    in_specs += [pl.BlockSpec(b.shape, lambda i, t: (0, 0)) for _, _, b in entries] + [whole] * (acc is not None)
    operands = [fisher] * len(entries) + [b for _, _, b in entries] + ([acc] if acc is not None else [])
    return pl.pallas_call(
        functools.partial(precond_kernel, len(entries), acc is not None),
        out_shape=jax.ShapeDtypeStruct((depth, width), dtype),
        grid_spec=pltpu.PrefetchScalarGridSpec(num_scalar_prefetch=1, grid=(1,), in_specs=in_specs, out_specs=whole),
        compiler_params=pltpu.CompilerParams(vmem_limit_bytes=VMEM_LIMIT),
        cost_estimate=pl.CostEstimate(
            flops=2 * depth * depth * width * len(entries),
            bytes_accessed=depth * (depth + 2 * width) * 2 * len(entries),
            transcendentals=0,
        ),
    )(table, *operands)


def place_kernel(table, order, docs, out):
    del table
    rows = order.shape[1]
    put = jnp.where(order[...] == lax.broadcasted_iota(jnp.int32, (rows, rows), 0), 1.0, 0.0).astype(jnp.bfloat16)
    out[...] = dot(put, docs[0]).astype(out.dtype)


def place(table, order, docs, depth, m):
    _, rows, width = docs.shape
    return pl.pallas_call(
        place_kernel,
        out_shape=jax.ShapeDtypeStruct((rows, width), docs.dtype),
        grid_spec=pltpu.PrefetchScalarGridSpec(
            num_scalar_prefetch=1,
            grid=(width // depth,),
            in_specs=[
                pl.BlockSpec((1, rows), lambda i, t: (0, 0)),
                pl.BlockSpec((1, rows, depth), lambda i, t: (m, 0, t[i])),
            ],
            out_specs=pl.BlockSpec((rows, depth), lambda i, t: (0, i)),
        ),
        compiler_params=pltpu.CompilerParams(vmem_limit_bytes=VMEM_LIMIT),
        cost_estimate=pl.CostEstimate(flops=2 * rows * rows * width, bytes_accessed=4 * rows * width, transcendentals=0),
    )(table, order, docs)


def per_device_plane(queries, inverse_fisher, documents, doc_order):
    fisher = inverse_fisher[0]
    modules, depth, width = fisher.shape
    n = width // depth
    ring = ring_order(n)
    up = [(ring[i], ring[(i + 1) % n]) for i in range(n)]
    down = [(b, a) for a, b in up]
    owners = np.zeros((n, n), np.int32)
    for i, d in enumerate(ring):
        owners[d] = [ring[(i - shift) % n] for shift in range(n)]
    table = jnp.asarray(owners)[lax.axis_index("doc")]
    docs = jnp.swapaxes(documents[0], 0, 1)

    def ring_gather(blocks, state, use, waits):
        going = [[block, block] for block in blocks]
        fresh = [[(0, 0, block)] for block in blocks]
        final = []
        for step in range(1, n // 2 + 1):
            for m in range(modules):
                if step > 1:
                    going[m], state[m], _ = lax.optimization_barrier((going[m], state[m], waits.get((step, m), ())))
                ways = going[m]
                if step == n // 2:
                    half = ways[0].shape[0] // 2
                    ways = [ways[0][:half], ways[1][half:]]
                going[m] = [lax.ppermute(ways[0], "doc", up), lax.ppermute(ways[1], "doc", down)]
                arrivals = [(step, 0, going[m][0]), (n - step, step // (n // 2), going[m][1])]
                if step < n // 2:
                    state[m] = use(m, state[m], fresh[m], False)
                    fresh[m] = arrivals
                else:
                    final.append(arrivals)
        for m in range(modules):
            if m > 0:
                blocks, _ = lax.optimization_barrier(([block for _, _, block in fresh[m]], state[m - 1]))
                fresh[m] = [(shift, half, block) for (shift, half, _), block in zip(fresh[m], blocks)]
            state[m] = use(m, use(m, state[m], fresh[m], False), final[m], True)
        return state

    def add_query(m, acc, arrivals, last):
        return add_precond(table, fisher, m, arrivals, acc, jnp.bfloat16 if last else jnp.float32)

    blocks = [queries[0, 0]]
    for m in range(1, modules):
        blocks.append(lax.optimization_barrier((queries, blocks[-1]))[0][0, m])
    placed = [place(table, doc_order, docs, depth, m) for m in range(modules)]
    waits = {(2, modules - 1): docs, (3, 0): placed[0], (3, modules - 1): placed[1:]}
    precond = ring_gather(blocks, [None] * modules, add_query, waits)

    def add_score(m, score, arrivals, last):
        for shift, half, block in arrivals:
            rows = block.shape[0]
            start = shift * depth + half * rows
            part = dot(placed[m][:, start : start + rows], block)
            score = part if score is None else score + part
        return score

    score = sum(ring_gather(precond, [None] * modules, add_score, {}))
    return score + lax.ppermute(score, "layer", [(0, 1), (1, 0)])


def per_device_any(queries, inverse_fisher, documents, doc_order):
    fisher = inverse_fisher[0]
    n_rows = documents.shape[1]
    put = (doc_order == lax.broadcasted_iota(jnp.int32, (n_rows, n_rows), 0)).astype(documents.dtype)
    placed = dot(put, documents[0].reshape(n_rows, -1)).astype(documents.dtype)
    full_queries = lax.all_gather(queries[0], "doc", axis=1, tiled=True)
    precond = jnp.einsum("mji,miq->mjq", fisher, full_queries, preferred_element_type=jnp.float32).astype(jnp.bfloat16)
    full_precond = lax.all_gather(precond, "doc", axis=1, tiled=True)
    score = dot(placed, full_precond.reshape(-1, full_precond.shape[2]))
    return lax.psum(score, "layer")


def solution(mesh):
    plane = mesh.shape["doc"] == 8 and mesh.shape["layer"] == 2
    in_specs = (
        P("layer", None, "doc", "groups"),
        P("layer", None, "doc", None),
        P("layer", ("groups", "doc"), None, None),
        P(("groups", "doc"), None),
    )
    return jax.shard_map(
        per_device_plane if plane else per_device_any,
        mesh=mesh,
        in_specs=in_specs,
        out_specs=P(("groups", "doc"), None),
        check_vma=False,
    )
```

```python
import functools

import jax
import jax.numpy as jnp
import numpy as np
from jax import lax
from jax.experimental import pallas as pl
from jax.experimental.pallas import tpu as pltpu
from jax.sharding import PartitionSpec as P

VMEM_LIMIT = 16 * 1024 * 1024


def dot(a, b):
    return jnp.dot(a, b, preferred_element_type=jnp.float32)


def ring_order(n):
    half = n // 2
    return [2 * i for i in range(half)] + [2 * i + 1 for i in reversed(range(half))]


def precond_kernel(count, has_acc, table, *refs):
    del table
    fisher, blocks = refs[:count], refs[count : 2 * count]
    total = refs[2 * count][...] if has_acc else None
    out = refs[-1]
    for f, block in zip(fisher, blocks):
        part = dot(f[0], block[...])
        total = part if total is None else total + part
    out[...] = total.astype(out.dtype)


def add_precond(table, fisher, m, entries, acc, dtype):
    _, depth, _ = fisher.shape
    width = entries[0][2].shape[1]
    whole = pl.BlockSpec((depth, width), lambda i, t: (0, 0))
    in_specs = [
        pl.BlockSpec((1, depth, b.shape[0]), lambda i, t, k=k, h=h, parts=depth // b.shape[0]: (m, 0, t[k] * parts + h))
        for k, h, b in entries
    ]
    in_specs += [pl.BlockSpec(b.shape, lambda i, t: (0, 0)) for _, _, b in entries] + [whole] * (acc is not None)
    operands = [fisher] * len(entries) + [b for _, _, b in entries] + ([acc] if acc is not None else [])
    return pl.pallas_call(
        functools.partial(precond_kernel, len(entries), acc is not None),
        out_shape=jax.ShapeDtypeStruct((depth, width), dtype),
        grid_spec=pltpu.PrefetchScalarGridSpec(num_scalar_prefetch=1, grid=(1,), in_specs=in_specs, out_specs=whole),
        compiler_params=pltpu.CompilerParams(vmem_limit_bytes=VMEM_LIMIT),
        cost_estimate=pl.CostEstimate(
            flops=2 * depth * depth * width * len(entries),
            bytes_accessed=depth * (depth + 2 * width) * 2 * len(entries),
            transcendentals=0,
        ),
    )(table, *operands)


def place_kernel(table, order, docs, out):
    del table
    rows = order.shape[1]
    put = jnp.where(order[...] == lax.broadcasted_iota(jnp.int32, (rows, rows), 0), 1.0, 0.0).astype(jnp.bfloat16)
    out[...] = dot(put, docs[0]).astype(out.dtype)


def place(table, order, docs, depth, m):
    _, rows, width = docs.shape
    return pl.pallas_call(
        place_kernel,
        out_shape=jax.ShapeDtypeStruct((rows, width), docs.dtype),
        grid_spec=pltpu.PrefetchScalarGridSpec(
            num_scalar_prefetch=1,
            grid=(width // depth,),
            in_specs=[
                pl.BlockSpec((1, rows), lambda i, t: (0, 0)),
                pl.BlockSpec((1, rows, depth), lambda i, t: (m, 0, t[i])),
            ],
            out_specs=pl.BlockSpec((rows, depth), lambda i, t: (0, i)),
        ),
        compiler_params=pltpu.CompilerParams(vmem_limit_bytes=VMEM_LIMIT),
        cost_estimate=pl.CostEstimate(flops=2 * rows * rows * width, bytes_accessed=4 * rows * width, transcendentals=0),
    )(table, order, docs)


def per_device_plane(queries, inverse_fisher, documents, doc_order):
    fisher = inverse_fisher[0]
    modules, depth, width = fisher.shape
    n = width // depth
    ring = ring_order(n)
    up = [(ring[i], ring[(i + 1) % n]) for i in range(n)]
    down = [(b, a) for a, b in up]
    owners = np.zeros((n, n), np.int32)
    for i, d in enumerate(ring):
        owners[d] = [ring[(i - shift) % n] for shift in range(n)]
    table = jnp.asarray(owners)[lax.axis_index("doc")]
    docs = jnp.swapaxes(documents[0], 0, 1)

    def ring_gather(blocks, state, use, waits):
        going = [[block, block] for block in blocks]
        fresh = [[(0, 0, block)] for block in blocks]
        final = []
        for step in range(1, n // 2 + 1):
            for m in range(modules):
                if step > 1:
                    ways = going[m] if step < n // 2 else going[m][:1]
                    ways, state[m], _ = lax.optimization_barrier((ways, state[m], waits.get((step, m), ())))
                    going[m] = ways + going[m][len(ways) :]
                ways = going[m]
                if step == n // 2:
                    half = ways[0].shape[0] // 2
                    ways = [ways[0][:half], ways[1][half:]]
                going[m] = [lax.ppermute(ways[0], "doc", up), lax.ppermute(ways[1], "doc", down)]
                arrivals = [(step, 0, going[m][0]), (n - step, step // (n // 2), going[m][1])]
                if step < n // 2:
                    state[m] = use(m, state[m], fresh[m], False)
                    fresh[m] = arrivals
                else:
                    final.append(arrivals)
        for m in range(modules):
            if m > 0:
                blocks, _ = lax.optimization_barrier(([block for _, _, block in fresh[m]], state[m - 1]))
                fresh[m] = [(shift, half, block) for (shift, half, _), block in zip(fresh[m], blocks)]
            state[m] = use(m, use(m, state[m], fresh[m], False), final[m], True)
        return state

    def add_query(m, acc, arrivals, last):
        return add_precond(table, fisher, m, arrivals, acc, jnp.bfloat16 if last else jnp.float32)

    blocks = [queries[0, 0]]
    for m in range(1, modules):
        blocks.append(lax.optimization_barrier((queries, blocks[-1]))[0][0, m])
    placed = [place(table, doc_order, docs, depth, m) for m in range(modules)]
    waits = {(2, modules - 1): docs, (3, 0): placed[0], (3, modules - 1): placed[1:]}
    precond = ring_gather(blocks, [None] * modules, add_query, waits)

    def add_score(m, score, arrivals, last):
        for shift, half, block in arrivals:
            rows = block.shape[0]
            start = shift * depth + half * rows
            part = dot(placed[m][:, start : start + rows], block)
            score = part if score is None else score + part
        return score

    score = sum(ring_gather(precond, [None] * modules, add_score, {}))
    return score + lax.ppermute(score, "layer", [(0, 1), (1, 0)])


def per_device_any(queries, inverse_fisher, documents, doc_order):
    fisher = inverse_fisher[0]
    n_rows = documents.shape[1]
    put = (doc_order == lax.broadcasted_iota(jnp.int32, (n_rows, n_rows), 0)).astype(documents.dtype)
    placed = dot(put, documents[0].reshape(n_rows, -1)).astype(documents.dtype)
    full_queries = lax.all_gather(queries[0], "doc", axis=1, tiled=True)
    precond = jnp.einsum("mji,miq->mjq", fisher, full_queries, preferred_element_type=jnp.float32).astype(jnp.bfloat16)
    full_precond = lax.all_gather(precond, "doc", axis=1, tiled=True)
    score = dot(placed, full_precond.reshape(-1, full_precond.shape[2]))
    return lax.psum(score, "layer")


def solution(mesh):
    plane = mesh.shape["doc"] == 8 and mesh.shape["layer"] == 2
    in_specs = (
        P("layer", None, "doc", "groups"),
        P("layer", None, "doc", None),
        P("layer", ("groups", "doc"), None, None),
        P(("groups", "doc"), None),
    )
    return jax.shard_map(
        per_device_plane if plane else per_device_any,
        mesh=mesh,
        in_specs=in_specs,
        out_specs=P(("groups", "doc"), None),
        check_vma=False,
    )
```

```python
import functools

import jax
import jax.numpy as jnp
import numpy as np
from jax import lax
from jax.experimental import pallas as pl
from jax.experimental.pallas import tpu as pltpu
from jax.sharding import PartitionSpec as P

VMEM_LIMIT = 16 * 1024 * 1024


def dot(a, b):
    return jnp.dot(a, b, preferred_element_type=jnp.float32)


def ring_order(n):
    half = n // 2
    return [2 * i for i in range(half)] + [2 * i + 1 for i in reversed(range(half))]


def precond_kernel(count, has_acc, table, *refs):
    del table
    fisher, blocks = refs[:count], refs[count : 2 * count]
    total = refs[2 * count][...] if has_acc else None
    out = refs[-1]
    for f, block in zip(fisher, blocks):
        part = dot(f[0], block[...])
        total = part if total is None else total + part
    out[...] = total.astype(out.dtype)


def add_precond(table, fisher, m, entries, acc, dtype):
    _, depth, _ = fisher.shape
    width = entries[0][2].shape[1]
    whole = pl.BlockSpec((depth, width), lambda i, t: (0, 0))
    in_specs = [
        pl.BlockSpec((1, depth, b.shape[0]), lambda i, t, k=k, part=row // b.shape[0], parts=depth // b.shape[0]: (m, 0, t[k] * parts + part))
        for k, row, b in entries
    ]
    in_specs += [pl.BlockSpec(b.shape, lambda i, t: (0, 0)) for _, _, b in entries] + [whole] * (acc is not None)
    operands = [fisher] * len(entries) + [b for _, _, b in entries] + ([acc] if acc is not None else [])
    return pl.pallas_call(
        functools.partial(precond_kernel, len(entries), acc is not None),
        out_shape=jax.ShapeDtypeStruct((depth, width), dtype),
        grid_spec=pltpu.PrefetchScalarGridSpec(num_scalar_prefetch=1, grid=(1,), in_specs=in_specs, out_specs=whole),
        compiler_params=pltpu.CompilerParams(vmem_limit_bytes=VMEM_LIMIT),
        cost_estimate=pl.CostEstimate(
            flops=2 * depth * depth * width * len(entries),
            bytes_accessed=depth * (depth + 2 * width) * 2 * len(entries),
            transcendentals=0,
        ),
    )(table, *operands)


def place_kernel(table, order, docs, out):
    del table
    rows = order.shape[1]
    put = jnp.where(order[...] == lax.broadcasted_iota(jnp.int32, (rows, rows), 0), 1.0, 0.0).astype(jnp.bfloat16)
    out[...] = dot(put, docs[0]).astype(out.dtype)


def place(table, order, docs, depth, m):
    _, rows, width = docs.shape
    return pl.pallas_call(
        place_kernel,
        out_shape=jax.ShapeDtypeStruct((rows, width), docs.dtype),
        grid_spec=pltpu.PrefetchScalarGridSpec(
            num_scalar_prefetch=1,
            grid=(width // depth,),
            in_specs=[
                pl.BlockSpec((1, rows), lambda i, t: (0, 0)),
                pl.BlockSpec((1, rows, depth), lambda i, t: (m, 0, t[i])),
            ],
            out_specs=pl.BlockSpec((rows, depth), lambda i, t: (0, i)),
        ),
        compiler_params=pltpu.CompilerParams(vmem_limit_bytes=VMEM_LIMIT),
        cost_estimate=pl.CostEstimate(flops=2 * rows * rows * width, bytes_accessed=4 * rows * width, transcendentals=0),
    )(table, order, docs)


def per_device_plane(queries, inverse_fisher, documents, doc_order):
    fisher = inverse_fisher[0]
    modules, depth, width = fisher.shape
    n = width // depth
    ring = ring_order(n)
    up = [(ring[i], ring[(i + 1) % n]) for i in range(n)]
    down = [(b, a) for a, b in up]
    owners = np.zeros((n, n), np.int32)
    for i, d in enumerate(ring):
        owners[d] = [ring[(i - shift) % n] for shift in range(n)]
    table = jnp.asarray(owners)[lax.axis_index("doc")]
    docs = jnp.swapaxes(documents[0], 0, 1)

    def ring_gather(blocks, state, use, waits, cuts):
        going = [[block, block] for block in blocks]
        fresh = [[(0, 0, block)] for block in blocks]
        final = []
        for step in range(1, n // 2 + 1):
            for m in range(modules):
                if step > 1:
                    ways = going[m] if step < n // 2 else going[m][:1]
                    ways, state[m], _ = lax.optimization_barrier((ways, state[m], waits.get((step, m), ())))
                    going[m] = ways + going[m][len(ways) :]
                ways = going[m]
                if step == n // 2:
                    ways = [ways[0][: cuts[m]], ways[1][cuts[m] :]]
                going[m] = [lax.ppermute(ways[0], "doc", up), lax.ppermute(ways[1], "doc", down)]
                arrivals = [(step, 0, going[m][0]), (n - step, cuts[m] * (step // (n // 2)), going[m][1])]
                if step < n // 2:
                    state[m] = use(m, state[m], fresh[m], False)
                    fresh[m] = arrivals
                else:
                    final.append(arrivals)
        for m in range(modules):
            if m > 0:
                blocks, _ = lax.optimization_barrier(([block for _, _, block in fresh[m]], state[m - 1]))
                fresh[m] = [(shift, row, block) for (shift, row, _), block in zip(fresh[m], blocks)]
            state[m] = use(m, use(m, state[m], fresh[m], False), final[m], True)
        return state

    def add_query(m, acc, arrivals, last):
        return add_precond(table, fisher, m, arrivals, acc, jnp.bfloat16 if last else jnp.float32)

    blocks = [queries[0, 0]]
    for m in range(1, modules):
        blocks.append(lax.optimization_barrier((queries, blocks[-1]))[0][0, m])
    placed = [place(table, doc_order, docs, depth, m) for m in range(modules)]
    waits = {(2, modules - 1): docs, (3, 0): placed[0], (3, modules - 1): placed[1:]}
    precond = ring_gather(blocks, [None] * modules, add_query, waits, [depth // 2] * modules)

    def add_score(m, score, arrivals, last):
        for shift, row, block in arrivals:
            start = shift * depth + row
            part = dot(placed[m][:, start : start + block.shape[0]], block)
            score = part if score is None else score + part
        return score

    cuts = [depth // 2] * (modules - 1) + [depth * 5 // 8]
    score = sum(ring_gather(precond, [None] * modules, add_score, {}, cuts))
    return score + lax.ppermute(score, "layer", [(0, 1), (1, 0)])


def per_device_any(queries, inverse_fisher, documents, doc_order):
    fisher = inverse_fisher[0]
    n_rows = documents.shape[1]
    put = (doc_order == lax.broadcasted_iota(jnp.int32, (n_rows, n_rows), 0)).astype(documents.dtype)
    placed = dot(put, documents[0].reshape(n_rows, -1)).astype(documents.dtype)
    full_queries = lax.all_gather(queries[0], "doc", axis=1, tiled=True)
    precond = jnp.einsum("mji,miq->mjq", fisher, full_queries, preferred_element_type=jnp.float32).astype(jnp.bfloat16)
    full_precond = lax.all_gather(precond, "doc", axis=1, tiled=True)
    score = dot(placed, full_precond.reshape(-1, full_precond.shape[2]))
    return lax.psum(score, "layer")


def solution(mesh):
    plane = mesh.shape["doc"] == 8 and mesh.shape["layer"] == 2
    in_specs = (
        P("layer", None, "doc", "groups"),
        P("layer", None, "doc", None),
        P("layer", ("groups", "doc"), None, None),
        P(("groups", "doc"), None),
    )
    return jax.shard_map(
        per_device_plane if plane else per_device_any,
        mesh=mesh,
        in_specs=in_specs,
        out_specs=P(("groups", "doc"), None),
        check_vma=False,
    )
```

```python
import functools

import jax
import jax.numpy as jnp
import numpy as np
from jax import lax
from jax.experimental import pallas as pl
from jax.experimental.pallas import tpu as pltpu
from jax.sharding import PartitionSpec as P

VMEM_LIMIT = 16 * 1024 * 1024


def dot(a, b):
    return jnp.dot(a, b, preferred_element_type=jnp.float32)


def ring_order(n):
    half = n // 2
    return [2 * i for i in range(half)] + [2 * i + 1 for i in reversed(range(half))]


def precond_kernel(count, has_acc, table, *refs):
    del table
    fisher, blocks = refs[:count], refs[count : 2 * count]
    total = refs[2 * count][...] if has_acc else None
    out = refs[-1]
    for f, block in zip(fisher, blocks):
        part = dot(f[0], block[...])
        total = part if total is None else total + part
    out[...] = total.astype(out.dtype)


def add_precond(table, fisher, m, entries, acc, dtype):
    _, depth, _ = fisher.shape
    width = entries[0][2].shape[1]
    whole = pl.BlockSpec((depth, width), lambda i, t: (0, 0))
    in_specs = [
        pl.BlockSpec((1, depth, b.shape[0]), lambda i, t, k=k, part=row // b.shape[0], parts=depth // b.shape[0]: (m, 0, t[k] * parts + part))
        for k, row, b in entries
    ]
    in_specs += [pl.BlockSpec(b.shape, lambda i, t: (0, 0)) for _, _, b in entries] + [whole] * (acc is not None)
    operands = [fisher] * len(entries) + [b for _, _, b in entries] + ([acc] if acc is not None else [])
    return pl.pallas_call(
        functools.partial(precond_kernel, len(entries), acc is not None),
        out_shape=jax.ShapeDtypeStruct((depth, width), dtype),
        grid_spec=pltpu.PrefetchScalarGridSpec(num_scalar_prefetch=1, grid=(1,), in_specs=in_specs, out_specs=whole),
        compiler_params=pltpu.CompilerParams(vmem_limit_bytes=VMEM_LIMIT),
        cost_estimate=pl.CostEstimate(
            flops=2 * depth * depth * width * len(entries),
            bytes_accessed=depth * (depth + 2 * width) * 2 * len(entries),
            transcendentals=0,
        ),
    )(table, *operands)


def place_kernel(table, order, docs, out):
    del table
    rows = order.shape[1]
    put = jnp.where(order[...] == lax.broadcasted_iota(jnp.int32, (rows, rows), 0), 1.0, 0.0).astype(jnp.bfloat16)
    out[...] = dot(put, docs[0]).astype(out.dtype)


def place(table, order, docs, depth, m):
    _, rows, width = docs.shape
    return pl.pallas_call(
        place_kernel,
        out_shape=jax.ShapeDtypeStruct((rows, width), docs.dtype),
        grid_spec=pltpu.PrefetchScalarGridSpec(
            num_scalar_prefetch=1,
            grid=(width // depth,),
            in_specs=[
                pl.BlockSpec((1, rows), lambda i, t: (0, 0)),
                pl.BlockSpec((1, rows, depth), lambda i, t: (m, 0, t[i])),
            ],
            out_specs=pl.BlockSpec((rows, depth), lambda i, t: (0, i)),
        ),
        compiler_params=pltpu.CompilerParams(vmem_limit_bytes=VMEM_LIMIT),
        cost_estimate=pl.CostEstimate(flops=2 * rows * rows * width, bytes_accessed=4 * rows * width, transcendentals=0),
    )(table, order, docs)


def per_device_plane(queries, inverse_fisher, documents, doc_order):
    fisher = inverse_fisher[0]
    modules, depth, width = fisher.shape
    n = width // depth
    ring = ring_order(n)
    up = [(ring[i], ring[(i + 1) % n]) for i in range(n)]
    down = [(b, a) for a, b in up]
    owners = np.zeros((n, n), np.int32)
    for i, d in enumerate(ring):
        owners[d] = [ring[(i - shift) % n] for shift in range(n)]
    table = jnp.asarray(owners)[lax.axis_index("doc")]
    docs = jnp.swapaxes(documents[0], 0, 1)

    def ring_gather(blocks, state, use, waits, cuts):
        going = [[block, block] for block in blocks]
        fresh = [[(0, 0, block)] for block in blocks]
        final = []
        for step in range(1, n // 2 + 1):
            for m in range(modules):
                if step > 1:
                    ways = going[m] if step < n // 2 or m < modules - 1 else going[m][:1]
                    ways, state[m], _ = lax.optimization_barrier((ways, state[m], waits.get((step, m), ())))
                    going[m] = ways + going[m][len(ways) :]
                ways = going[m]
                if step == n // 2:
                    ways = [ways[0][: cuts[m]], ways[1][cuts[m] :]]
                going[m] = [lax.ppermute(ways[0], "doc", up), lax.ppermute(ways[1], "doc", down)]
                arrivals = [(step, 0, going[m][0]), (n - step, cuts[m] * (step // (n // 2)), going[m][1])]
                if step < n // 2:
                    state[m] = use(m, state[m], fresh[m], False)
                    fresh[m] = arrivals
                else:
                    final.append(arrivals)
        for m in range(modules):
            if m > 0:
                blocks, _ = lax.optimization_barrier(([block for _, _, block in fresh[m]], state[m - 1]))
                fresh[m] = [(shift, row, block) for (shift, row, _), block in zip(fresh[m], blocks)]
            state[m] = use(m, use(m, state[m], fresh[m], False), final[m], True)
        return state

    def add_query(m, acc, arrivals, last):
        return add_precond(table, fisher, m, arrivals, acc, jnp.bfloat16 if last else jnp.float32)

    blocks = [queries[0, 0]]
    for m in range(1, modules):
        blocks.append(lax.optimization_barrier((queries, blocks[-1]))[0][0, m])
    placed = [place(table, doc_order, docs, depth, m) for m in range(modules)]
    waits = {(2, modules - 1): docs, (3, 0): placed[0], (3, modules - 1): placed[1:]}
    precond = ring_gather(blocks, [None] * modules, add_query, waits, [depth // 2] * modules)

    def add_score(m, score, arrivals, last):
        for shift, row, block in arrivals:
            start = shift * depth + row
            part = dot(placed[m][:, start : start + block.shape[0]], block)
            score = part if score is None else score + part
        return score

    cuts = [depth // 2] * (modules - 1) + [depth * 5 // 8]
    score = sum(ring_gather(precond, [None] * modules, add_score, {}, cuts))
    return score + lax.ppermute(score, "layer", [(0, 1), (1, 0)])


def per_device_any(queries, inverse_fisher, documents, doc_order):
    fisher = inverse_fisher[0]
    n_rows = documents.shape[1]
    put = (doc_order == lax.broadcasted_iota(jnp.int32, (n_rows, n_rows), 0)).astype(documents.dtype)
    placed = dot(put, documents[0].reshape(n_rows, -1)).astype(documents.dtype)
    full_queries = lax.all_gather(queries[0], "doc", axis=1, tiled=True)
    precond = jnp.einsum("mji,miq->mjq", fisher, full_queries, preferred_element_type=jnp.float32).astype(jnp.bfloat16)
    full_precond = lax.all_gather(precond, "doc", axis=1, tiled=True)
    score = dot(placed, full_precond.reshape(-1, full_precond.shape[2]))
    return lax.psum(score, "layer")


def solution(mesh):
    plane = mesh.shape["doc"] == 8 and mesh.shape["layer"] == 2
    in_specs = (
        P("layer", None, "doc", "groups"),
        P("layer", None, "doc", None),
        P("layer", ("groups", "doc"), None, None),
        P(("groups", "doc"), None),
    )
    return jax.shard_map(
        per_device_plane if plane else per_device_any,
        mesh=mesh,
        in_specs=in_specs,
        out_specs=P(("groups", "doc"), None),
        check_vma=False,
    )
```
